32 devices in a mesh: dp: 2 (over x), space: 16 (over z, y, core).
Axes of the slice: x: 2, y: 2, z: 4, core: 2. Of those that a mesh axis runs over, the one named last changes fastest.
Arguments:
- fields: bfloat16 [2, 64, 32, 32, 128], P('dp', 'space'), may hold values from -6 to 6
- cotangent: bfloat16 [2, 64, 32, 32, 128], P('dp', 'space'), may hold values from -6 to 6
- w_first: bfloat16 [3, 3, 128, 128], replicated, may hold values from -0.1875 to 0.1875
- w_second: bfloat16 [3, 3, 128, 128], replicated, may hold values from -0.1875 to 0.1875
- tile_links: int32 [64, 4, 5], P('space'), may hold values from 0 to 63, as said below
Outputs:
- mixed: bfloat16 [2, 64, 32, 32, 128], P('dp', 'space')
- grad_first: float32 [3, 3, 128, 128], replicated
- grad_second: float32 [3, 3, 128, 128], replicated
The draws below stay inside these ranges and needn't reach their ends.
Inputs may be any that keep to these rules, and one draw needn't show every extreme that they name: `tile_links`: columns 0 and 3 are tile numbers; columns 1 and 4 are an edge or corner 0 to 3; column 2 is 0 or 1. The links are mutual: if side k of tile t reads edge e of tile u with flag f, side e of u reads edge k of t with flag f; if corner k of t reads corner q of u, corner q of u reads corner k of t. Tiles 4 * d to 4 * d + 3 lie on index d of space; every source of a tile lies on its index, the next or the previous one, the last index being next to the first. Only the first 4 tiles of an index read from the previous index and only the last 4 from the next, each through exactly one side and the two corners at that side's ends; each tile read there is read through a side by exactly one tile of the reading index, and the corners read from it are the ends of that edge.
All inputs are finite; a program needn't handle non-finite values.
Results may differ from the reference program's by a relative error of at most 0.0031.
Values may be sent and summed in bfloat16 or wider, within the bound.
A program may use at most 64 MiB of HBM per device.

```python
import jax
import jax.numpy as jnp
from jax import lax

C = 128
S = 32
BAND = 4
TILES = 64
SAMPLES = 2


def draw_tile_links(key, part):
    rotation = jax.random.randint(jax.random.fold_in(key, 11), (TILES,), 0, 4).astype(jnp.int32)
    tile_ids = jnp.arange(TILES, dtype=jnp.int32)
    line_count = TILES // BAND
    line_of = tile_ids // BAND
    column_of = tile_ids % BAND
    quarter = jnp.arange(4, dtype=jnp.int32)
    layout = (quarter[None, :] - rotation[:, None]) % 4
    side_line = jnp.where(layout == 0, -1, jnp.where(layout == 2, 1, 0))
    side_column = jnp.where(layout == 1, 1, jnp.where(layout == 3, -1, 0))
    side_source = (line_of[:, None] + side_line) % line_count * BAND + (column_of[:, None] + side_column) % BAND
    side_edge = ((layout + 2) % 4 + rotation[side_source]) % 4
    side_rev = ((quarter[None, :] < 2) == (side_edge < 2)).astype(jnp.int32)
    corner_line = jnp.where(layout < 2, -1, 1)
    corner_column = jnp.where((layout == 0) | (layout == 3), -1, 1)
    corner_source = (line_of[:, None] + corner_line) % line_count * BAND + (column_of[:, None] + corner_column) % BAND
    corner_at = ((layout + 2) % 4 + rotation[corner_source]) % 4
    return jnp.stack([side_source, side_edge, side_rev, corner_source, corner_at], axis=-1).astype(jnp.int32)


def block_scale(rng, shape, pieces, low, largest):
    def one(position, blocks):
        draws = jax.random.uniform(jax.random.fold_in(jax.random.fold_in(rng, 6), position), (blocks,), jnp.float32, low / len(pieces), largest / len(pieces))
        return jnp.repeat(jnp.exp(draws), shape[position] // blocks).reshape((-1,) + (1,) * (len(shape) - position - 1))

    level = one(*pieces[0])
    for cut in pieces[1:]:
        level = level * one(*cut)
    return level


def bell_draw(own_key, dims, scale, reach, shards=(), held_as=jnp.bfloat16):
    factor_of = block_scale(own_key, dims, shards, -0.22, 0.18) if shards else 1.0
    values = jax.random.normal(own_key, dims, jnp.float32) * scale * factor_of
    return jnp.minimum(jnp.maximum(values, -reach), reach).astype(held_as)


def setup_inputs(seed: int = 0) -> dict:
    keys = jax.random.split(jax.random.key(seed), 6)
    fields = bell_draw(keys[0], (SAMPLES, TILES, S, S, C), 1.0, 6.0, ((0, 2), (1, 16)))
    cotangent = bell_draw(keys[1], (SAMPLES, TILES, S, S, C), 1.0, 6.0, ((0, 2), (1, 16)))
    w_first = bell_draw(keys[2], (3, 3, C, C), (9 * C) ** -0.5, 0.1875)
    w_second = bell_draw(keys[3], (3, 3, C, C), (9 * C) ** -0.5, 0.1875)
    tile_links = draw_tile_links(jax.random.fold_in(keys[5], 71), 0)
    return dict(fields=fields, cotangent=cotangent, w_first=w_first, w_second=w_second, tile_links=tile_links)


def edge_strips(values_in):
    extent = values_in.shape[-2]
    top_row = values_in[..., 0, :, :]
    right_col = values_in[..., :, extent - 1, :]
    bottom_row = values_in[..., extent - 1, :, :]
    left_col = values_in[..., :, 0, :]
    sides = jnp.stack([top_row, right_col, bottom_row, left_col], axis=-3)
    corner_pix = jnp.stack([values_in[..., 0, 0, :], values_in[..., 0, extent - 1, :], values_in[..., extent - 1, extent - 1, :], values_in[..., extent - 1, 0, :]], axis=-2)
    return jnp.concatenate([sides, corner_pix[..., None, :]], axis=-2)

def assemble(values_in, pool_rows, side_rows, side_flip, corner_rows):
    extent = values_in.shape[-2]
    picked = pool_rows[side_rows]
    ghosts = picked[:, :, :extent, :]
    ghosts = jnp.where(side_flip[:, :, None, None] == 1, ghosts[:, :, ::-1, :], ghosts)
    corner_pix = pool_rows[corner_rows][:, :, extent, :]
    middle = jnp.concatenate([ghosts[:, 3, :, None, :], values_in, ghosts[:, 1, :, None, :]], axis=2)
    top_line = jnp.concatenate([corner_pix[:, 0:1], ghosts[:, 0], corner_pix[:, 1:2]], axis=1)
    bottom_line = jnp.concatenate([corner_pix[:, 3:4], ghosts[:, 2], corner_pix[:, 2:3]], axis=1)
    return jnp.concatenate([top_line[:, None], middle, bottom_line[:, None]], axis=1)

def ghost_grads(padded_grad, side_flip):
    sides = jnp.stack([padded_grad[:, 0, 1:-1], padded_grad[:, 1:-1, -1], padded_grad[:, -1, 1:-1], padded_grad[:, 1:-1, 0]], axis=1)
    sides = jnp.where(side_flip[:, :, None, None] == 1, sides[:, :, ::-1, :], sides)
    corner_pix = jnp.stack([padded_grad[:, 0, 0], padded_grad[:, 0, -1], padded_grad[:, -1, -1], padded_grad[:, -1, 0]], axis=1)
    return (sides, corner_pix)

def add_edges(gradient, returned):
    extent = gradient.shape[1]
    gradient = gradient.at[:, 0, :, :].add(returned[:, 0, :extent])
    gradient = gradient.at[:, :, extent - 1, :].add(returned[:, 1, :extent])
    gradient = gradient.at[:, extent - 1, :, :].add(returned[:, 2, :extent])
    gradient = gradient.at[:, :, 0, :].add(returned[:, 3, :extent])
    gradient = gradient.at[:, 0, 0, :].add(returned[:, 0, extent])
    gradient = gradient.at[:, 0, extent - 1, :].add(returned[:, 1, extent])
    gradient = gradient.at[:, extent - 1, extent - 1, :].add(returned[:, 2, extent])
    gradient = gradient.at[:, extent - 1, 0, :].add(returned[:, 3, extent])
    return gradient

def conv_valid(padded, kernel):
    return lax.conv_general_dilated(padded, kernel, (1, 1), 'VALID', dimension_numbers=('NHWC', 'HWIO', 'NHWC'), preferred_element_type=jnp.float32)

def conv_back(cotan, kernel):
    flipped = jnp.transpose(kernel[::-1, ::-1], (0, 1, 3, 2))
    return lax.conv_general_dilated(cotan, flipped, (1, 1), ((2, 2), (2, 2)), dimension_numbers=('NHWC', 'HWIO', 'NHWC'), preferred_element_type=jnp.float32)

def kernel_grad(padded, cotan):
    extent = cotan.shape[1]
    width = cotan.shape[-1]
    flat_cot = cotan.reshape(-1, width)
    blocks = []
    for row_off in range(3):
        for col_off in range(3):
            window = padded[:, row_off:row_off + extent, col_off:col_off + extent, :].reshape(-1, width)
            blocks.append(lax.dot_general(window, flat_cot, (((0,), (0,)), ((), ())), preferred_element_type=jnp.float32))
    return jnp.stack(blocks).reshape(3, 3, width, width)

def reference(fields, cotangent, w_first, w_second, tile_links):
    side_rows = (tile_links[:, :, 0] * 4 + tile_links[:, :, 1]).astype(jnp.int32)
    side_flip = tile_links[:, :, 2]
    corner_rows = (tile_links[:, :, 3] * 4 + tile_links[:, :, 4]).astype(jnp.int32)

    def one_sample(pair):
        sample_in, cotan = pair
        pool_in = edge_strips(sample_in).reshape(TILES * 4, S + 1, C)
        padded_in = assemble(sample_in, pool_in, side_rows, side_flip, corner_rows)
        hidden = conv_valid(padded_in, w_first)
        gate = jax.nn.sigmoid(hidden)
        active = (hidden * gate).astype(jnp.bfloat16)
        pool_act = edge_strips(active).reshape(TILES * 4, S + 1, C)
        padded_act = assemble(active, pool_act, side_rows, side_flip, corner_rows)
        mixed = (sample_in.astype(jnp.float32) + conv_valid(padded_act, w_second)).astype(jnp.bfloat16)
        grad_second = kernel_grad(padded_act, cotan)
        padded_grad = conv_back(cotan, w_second)
        sides, corner_pix = ghost_grads(padded_grad, side_flip)
        pool_sides = jnp.zeros((TILES * 4, S, C), jnp.float32).at[side_rows.reshape(-1)].add(sides.reshape(-1, S, C))
        pool_corner = jnp.zeros((TILES * 4, C), jnp.float32).at[corner_rows.reshape(-1)].add(corner_pix.reshape(-1, C))
        returned = jnp.concatenate([pool_sides, pool_corner[:, None]], axis=1).reshape(TILES, 4, S + 1, C)
        active_grad = add_edges(padded_grad[:, 1:-1, 1:-1], returned)
        hidden_grad = (active_grad * gate * (1.0 + hidden * (1.0 - gate))).astype(jnp.bfloat16)
        grad_first = kernel_grad(padded_in, hidden_grad)
        return (mixed, grad_first, grad_second)
    mixed, grad_first, grad_second = lax.map(one_sample, (fields, cotangent))
    scale = float(SAMPLES * TILES * S * S) ** (-0.5)
    return (mixed, lax.optimization_barrier(jnp.sum(grad_first, axis=0)) * scale, lax.optimization_barrier(jnp.sum(grad_second, axis=0)) * scale)
```

```python
import functools

import jax
import jax.numpy as jnp
from jax import lax
from jax.experimental import pallas as pl
from jax.experimental.pallas import tpu as pltpu
from jax.sharding import PartitionSpec as P

F32 = jnp.float32
BF16 = jnp.bfloat16
MESH = pl.DeviceIdType.MESH
TRAVEL = (F32, F32, F32, F32)


def plan(dp_size, space_size, rows):
    mid = 2 if space_size % 4 == 0 else 1
    group = dp_size * mid
    far = space_size // (2 * mid)
    piece = -(-rows // (2 * group * 16)) * 16
    return mid, group, far, piece


def kernel(
    dp_size, space_size, tiles, side, chans, scale,
    links, f_ref, c_ref, w1_ref, w2_ref,
    mixed_ref, g1_ref, g2_ref,
    xc, ac, cc, gc, wb, deriv, agrad, rims, rim_corners,
    pool0, pool1, pool2, land0, land1, land2, out0, out1, out2,
    acc1, acc2, ra1, ra2, half1, half2, sb1, sb2, rb1, rb2, sc1, sc2, rc1, rc2, fo1, fo2,
    halo_send, halo_recv, red_send, red_recv,
):
    T, S, C = tiles, side, chans
    K = 3 * C
    pix = S * S
    pad_rows = S + 2
    su = S // 16
    own_units = 4 * T * su + T
    msg_units = T * su + T
    mid, group, far, piece = plan(dp_size, space_size, 9 * C)
    d = lax.axis_index("dp")
    s = lax.axis_index("space")
    core = lax.rem(s, 2)
    y = lax.rem(lax.div(s, 2), mid)
    z = lax.div(s, 2 * mid)
    b = d * mid + y
    lower = lax.rem(s + space_size - 1, space_size)
    upper = lax.rem(s + 1, space_size)
    partner = s + 1 - 2 * core

    def plane_peer(step):
        other = lax.rem(b + step, group)
        return (lax.div(other, mid), z * (2 * mid) + lax.rem(other, mid) * 2 + core)

    def far_peer(step):
        other = lax.rem(z + step, far)
        return (d, (other * mid + y) * 2 + core)

    barrier = pltpu.get_barrier_semaphore()
    greeted = [(d, lower), (d, upper), (d, partner)]
    greeted += [plane_peer(step) for step in range(1, group)]
    greeted += [far_peer(step) for step in range(1, far)]
    for peer in greeted:
        pl.semaphore_signal(barrier, inc=1, device_id=peer, device_id_type=MESH)

    def where_is(source):
        rel = lax.rem(lax.div(source, T) - s + 1 + space_size, space_size)
        return rel, lax.rem(source, T)

    strip_at, corner_at, face_lower, face_upper = {}, {}, [], []
    for t in range(T):
        low, up = 0, 0
        for k in range(4):
            rel, slot = where_is(links[t, k, 0])
            strip_at[t, k] = jnp.where(
                rel == 1,
                (slot * 4 + links[t, k, 1]) * su,
                jnp.where(rel == 0, own_units, own_units + msg_units) + slot * su,
            )
            low = low + jnp.where(rel == 0, k, 0)
            up = up + jnp.where(rel == 2, k, 0)
            rel, slot = where_is(links[t, k, 3])
            corner_at[t, k] = slot + jnp.where(
                rel == 1,
                4 * T * su,
                jnp.where(rel == 0, own_units, own_units + msg_units) + T * su,
            )
        face_lower.append(low)
        face_upper.append(up)

    row_id = lax.broadcasted_iota(jnp.int32, (S, S), 0)
    col_id = lax.broadcasted_iota(jnp.int32, (S, S), 1)
    same = (row_id == col_id).astype(F32)
    turned = (row_id + col_id == S - 1).astype(F32)
    unit_row = lax.broadcasted_iota(jnp.int32, (16, C), 0)
    line_row = lax.broadcasted_iota(jnp.int32, (S, C), 0)
    block_col = lax.broadcasted_iota(jnp.int32, (S, S, C), 1)

    pools, lands, outs = (pool0, pool1, pool2), (land0, land1, land2), (out0, out1, out2)

    def keep_strip(pool, t, k, strip):
        pool[pl.ds((t * 4 + k) * su, su)] = strip.astype(BF16).reshape(su, 16, C)

    def keep_corners(pool, t, corners):
        unit = jnp.zeros((16, C), F32)
        for k in range(4):
            unit = jnp.where(unit_row == k, corners[k], unit)
        pool[4 * T * su + t] = unit.astype(BF16)

    def keep_edges(pool, t, value):
        top, bottom = value[0], value[S - 1]
        keep_strip(pool, t, 0, top)
        keep_strip(pool, t, 1, value[:, S - 1, :])
        keep_strip(pool, t, 2, bottom)
        keep_strip(pool, t, 3, value[:, 0, :])
        keep_corners(pool, t, [top[0:1], top[S - 1 : S], bottom[S - 1 : S], bottom[0:1]])

    def halo_copies(which):
        copies = []
        for way, (peer, place) in enumerate(((lower, 1), (upper, 0))):
            copies.append(
                pltpu.make_async_remote_copy(
                    src_ref=outs[which].at[way],
                    dst_ref=lands[which].at[place],
                    send_sem=halo_send.at[which, way],
                    recv_sem=halo_recv.at[which, way],
                    device_id=(d, peer),
                    device_id_type=MESH,
                )
            )
        return copies

    def send_halo(which):
        pool, out = pools[which], outs[which]
        for way, faces in enumerate((face_lower, face_upper)):
            for t in range(T):
                out[way, pl.ds(t * su, su)] = pool[pl.ds((t * 4 + faces[t]) * su, su)]
                out[way, T * su + t] = pool[4 * T * su + t]

    def take_halo(which, copies):
        pool = pools[which]
        for copy in copies:
            copy.wait_recv()
        for place in range(2):
            pool[pl.ds(own_units + place * msg_units, msg_units)] = lands[which][place]
        for t in range(T):
            for k in range(4):
                strip = pool[pl.ds(strip_at[t, k], su)].reshape(S, C)
                flag = links[t, k, 2].astype(F32)
                turn = (flag * turned + (1.0 - flag) * same).astype(BF16)
                rims[t, k] = jnp.dot(turn, strip, preferred_element_type=F32)
                unit = pool[corner_at[t, k]].astype(F32)
                rim_corners[t, k] = jnp.broadcast_to(
                    jnp.sum(jnp.where(unit_row == links[t, k, 4], unit, 0.0), 0, keepdims=True),
                    (8, C),
                )

    def shifted(dst, t, at, value, left, right, columns):
        extent = columns.ndim - 2
        last = S - 1
        before = jnp.where(columns == 0, left, pltpu.roll(value, 1, axis=extent))
        after = jnp.where(columns == last, right, pltpu.roll(value, last, axis=extent))
        dst[t, at, :, 0:C] = before.astype(BF16)
        dst[t, at, :, C : 2 * C] = value.astype(BF16)
        dst[t, at, :, 2 * C : K] = after.astype(BF16)

    def fill_padded(dst, t, value):
        left, right = rims[t, 3], rims[t, 1]
        shifted(dst, t, pl.ds(1, S), value, left[:, None, :], right[:, None, :], block_col)
        tl, tr = rim_corners[t, 0, 0:1], rim_corners[t, 1, 0:1]
        br, bl = rim_corners[t, 2, 0:1], rim_corners[t, 3, 0:1]
        shifted(dst, t, 0, rims[t, 0], tl, tr, line_row)
        shifted(dst, t, S + 1, rims[t, 2], bl, br, line_row)

    def conv(src, t, kernel_rows, order):
        lhs = jnp.concatenate([src[t, r : r + S].reshape(pix, K) for r in order], axis=1)
        return jnp.dot(lhs, kernel_rows, preferred_element_type=F32)

    def lower_rows(t, value):
        zero = jnp.zeros((1, S, C), BF16)
        for r in range(3):
            lanes = slice(r * C, (r + 1) * C)
            gc[t, r : r + S, :, lanes] = value
            for at in range(r):
                gc[t, at : at + 1, :, lanes] = zero
            for at in range(r + S, pad_rows):
                gc[t, at : at + 1, :, lanes] = zero

    def kernel_grad(padded, acc):
        total = None
        for t in range(T):
            part = lax.dot_general(
                padded[t].reshape(pad_rows * S, K),
                gc[t].reshape(pad_rows * S, K),
                (((0,), (0,)), ((), ())),
                preferred_element_type=F32,
            )
            total = part if total is None else total + part
        for r in range(3):
            for c in range(3):
                acc[pl.ds((r * 3 + c) * C, C)] = total[c * C : (c + 1) * C, r * C : (r + 1) * C]
        if 2 * group * piece > 9 * C:
            acc[9 * C :] = jnp.zeros((2 * group * piece - 9 * C, C), F32)

    half_rows = group * piece
    stage_at = (0, 1, group, group + far - 1, 2 * group + far - 2)

    def remote(which, index, src, dst, peer):
        return pltpu.make_async_remote_copy(
            src_ref=src, dst_ref=dst,
            send_sem=red_send.at[which, index], recv_sem=red_recv.at[which, index],
            device_id=peer, device_id_type=MESH,
        )

    accs, ras, halves = (acc1, acc2), (ra1, ra2), (half1, half2)
    sbs, rbs, scs, rcs, fos = (sb1, sb2), (rb1, rb2), (sc1, sc2), (rc1, rc2), (fo1, fo2)
    pending = []

    def launch(copies):
        for copy in copies:
            copy.start()
        pending.extend(copies)
        return copies

    def landed(copies):
        for copy in copies:
            copy.wait_recv()

    def pair_start(g):
        src = accs[g].at[pl.ds((1 - core) * half_rows, half_rows)]
        return launch([remote(g, 0, src, ras[g], (d, partner))])

    def plane_start(g, copies):
        landed(copies)
        halves[g][...] = accs[g][pl.ds(core * half_rows, half_rows)] + ras[g][...]
        result = []
        for step in range(1, group):
            other = lax.rem(b + step, group)
            sbs[g][step - 1] = halves[g][pl.ds(other * piece, piece)].astype(sbs[g].dtype)
            result.append(
                remote(g, stage_at[1] + step - 1, sbs[g].at[step - 1], rbs[g].at[step - 1], plane_peer(step))
            )
        return launch(result)

    def far_start(g, copies):
        landed(copies)
        total = halves[g][pl.ds(b * piece, piece)]
        for step in range(1, group):
            total = total + rbs[g][step - 1].astype(F32)
        scs[g][...] = total.astype(scs[g].dtype)
        return launch([
            remote(g, stage_at[2] + step - 1, scs[g], rcs[g].at[z], far_peer(step))
            for step in range(1, far)
        ])

    def back_start(g, copies):
        landed(copies)
        total = jnp.zeros((piece, C), F32)
        mine = scs[g][...].astype(F32)
        for at in range(far):
            total = total + jnp.where(z == at, mine, rcs[g][at].astype(F32))
        fos[g][core, b] = (total * scale).astype(fos[g].dtype)
        spot = fos[g].at[core, b]
        return launch([
            remote(g, stage_at[3] + step - 1, spot, spot, plane_peer(step))
            for step in range(1, group)
        ])

    def pair_back(g, copies):
        landed(copies)
        spot = fos[g].at[core]
        return launch([remote(g, stage_at[4], spot, spot, (d, partner))])

    def finish(g, copies, out):
        landed(copies)
        out[...] = fos[g][...].reshape(2 * half_rows, C)[: 9 * C].astype(F32).reshape(3, 3, C, C)

    @pl.loop(0, T)
    def _(t):
        keep_edges(pool0, t, f_ref[0, t].astype(F32))

    send_halo(0)
    pl.semaphore_wait(barrier, len(greeted))
    copies0 = halo_copies(0)
    launch(copies0)

    for r in range(3):
        for c in range(3):
            wb[pl.ds((r * 3 + c) * C, C)] = w2_ref[r, c].astype(F32).T.astype(BF16)

    @pl.loop(0, T)
    def _(t):
        value = c_ref[0, t].astype(F32)
        blank = jnp.zeros((1, S, K), BF16)
        zero = jnp.zeros((), F32)
        up = jnp.where(block_col == S - 1, zero, pltpu.roll(value, S - 1, axis=1))
        down = jnp.where(block_col == 0, zero, pltpu.roll(value, 1, axis=1))
        cc[t, pl.ds(1, S), :, 0:C] = up.astype(BF16)
        cc[t, pl.ds(1, S), :, C : 2 * C] = c_ref[0, t]
        cc[t, pl.ds(1, S), :, 2 * C : K] = down.astype(BF16)
        cc[t, 0:1] = blank
        cc[t, S + 1 : S + 2] = blank
        top = jnp.dot(cc[t, 1], wb[0:K], preferred_element_type=F32)
        bottom = jnp.dot(cc[t, S], wb[2 * K : 3 * K], preferred_element_type=F32)
        corners = {}
        for column, c, k in ((0, 0, 3), (S - 1, 2, 1)):
            line = value[:, column, :].astype(BF16)
            parts = [
                jnp.dot(line, wb[(r * 3 + c) * C : (r * 3 + c + 1) * C], preferred_element_type=F32)
                for r in range(3)
            ]
            strip = parts[1]
            strip = strip + jnp.where(line_row == S - 1, 0.0, pltpu.roll(parts[0], S - 1, axis=0))
            strip = strip + jnp.where(line_row == 0, 0.0, pltpu.roll(parts[2], 1, axis=0))
            keep_strip(pool1, t, k, strip)
            corners[c] = (parts[0][0:1], parts[2][S - 1 : S])
        keep_strip(pool1, t, 0, top)
        keep_strip(pool1, t, 2, bottom)
        keep_corners(pool1, t, [corners[0][0], corners[2][0], corners[2][1], corners[0][1]])

    send_halo(1)
    copies1 = launch(halo_copies(1))

    @pl.loop(0, T)
    def _(t):
        agrad[t] = conv(cc, t, wb[...], (2, 1, 0)).reshape(S, S, C)

    take_halo(0, copies0)

    @pl.loop(0, T)
    def _(t):
        fill_padded(xc, t, f_ref[0, t].astype(F32))
        hidden = conv(xc, t, w1_ref[...].reshape(9 * C, C), (0, 1, 2))
        gate = jax.nn.sigmoid(hidden)
        active = (hidden * gate).reshape(S, S, C)
        deriv[t] = (gate * (1.0 + hidden * (1.0 - gate))).reshape(S, S, C)
        ac[t, pl.ds(1, S), :, C : 2 * C] = active.astype(BF16)
        keep_edges(pool2, t, active)

    send_halo(2)
    copies2 = launch(halo_copies(2))

    take_halo(1, copies1)

    @pl.loop(0, T)
    def _(t):
        agrad[t, 0] = agrad[t, 0] + rims[t, 0]
        agrad[t, S - 1] = agrad[t, S - 1] + rims[t, 2]
        for column, k, above, below in ((0, 3, 0, 3), (S - 1, 1, 1, 2)):
            strip = rims[t, k]
            strip = strip + jnp.where(line_row == 0, rim_corners[t, above, 0:1], 0.0)
            strip = strip + jnp.where(line_row == S - 1, rim_corners[t, below, 0:1], 0.0)
            agrad[t, :, column : column + 1, :] = (
                agrad[t, :, column : column + 1, :] + strip[:, None, :]
            )
        lower_rows(t, (agrad[t] * deriv[t]).astype(BF16))

    kernel_grad(xc, acc1)
    first = pair_start(0)

    take_halo(2, copies2)

    @pl.loop(0, T)
    def _(t):
        fill_padded(ac, t, ac[t, pl.ds(1, S), :, C : 2 * C].astype(F32))
        lower_rows(t, c_ref[0, t])

    first = plane_start(0, first)
    kernel_grad(ac, acc2)
    second = pair_start(1)
    first = far_start(0, first)

    def output(t):
        out = conv(ac, t, w2_ref[...].reshape(9 * C, C), (0, 1, 2)).reshape(S, S, C)
        mixed_ref[0, t] = (f_ref[0, t].astype(F32) + out).astype(BF16)

    pl.loop(0, T // 2)(output)
    second = plane_start(1, second)
    first = back_start(0, first)
    pl.loop(T // 2, T)(output)
    second = far_start(1, second)
    first = pair_back(0, first)
    second = back_start(1, second)
    finish(0, first, g1_ref)
    second = pair_back(1, second)
    finish(1, second, g2_ref)
    for copy in pending:
        copy.wait_send()


def block(mesh, fields, cotangent, w_first, w_second, tile_links):
    samples, T, S, _, C = fields.shape
    assert samples == 1
    dp_size, space_size = mesh.shape["dp"], mesh.shape["space"]
    mid, group, far, piece = plan(dp_size, space_size, 9 * C)
    scale = float(samples * dp_size * T * space_size * S * S) ** (-0.5)
    su = S // 16
    own_units, msg_units = 4 * T * su + T, T * su + T
    vmem = pltpu.VMEM
    padded = vmem((T, S + 2, S, 3 * C), BF16)
    twice = lambda shape, kind: [vmem(shape, kind), vmem(shape, kind)]
    stages = 2 * group + far - 1
    specs = pl.BlockSpec(memory_space=pltpu.VMEM)
    return pl.pallas_call(
        functools.partial(kernel, dp_size, space_size, T, S, C, scale),
        out_shape=(
            jax.ShapeDtypeStruct(fields.shape, BF16),
            jax.ShapeDtypeStruct(w_first.shape, F32),
            jax.ShapeDtypeStruct(w_second.shape, F32),
        ),
        in_specs=[pl.BlockSpec(memory_space=pltpu.SMEM), specs, specs, specs, specs],
        out_specs=(specs, specs, specs),
        scratch_shapes=[
            padded, padded, padded, padded,
            vmem((9 * C, C), BF16),
            vmem((T, S, S, C), F32),
            vmem((T, S, S, C), F32),
            vmem((T, 4, S, C), F32),
            vmem((T, 4, 8, C), F32),
        ]
        + [vmem((own_units + 2 * msg_units, 16, C), BF16)] * 3
        + [vmem((2, msg_units, 16, C), BF16)] * 6
        + twice((2 * group * piece, C), F32)
        + twice((group * piece, C), TRAVEL[0])
        + twice((group * piece, C), F32)
        + twice((group - 1, piece, C), TRAVEL[1])
        + twice((group - 1, piece, C), TRAVEL[1])
        + twice((piece, C), TRAVEL[2])
        + twice((far, piece, C), TRAVEL[2])
        + twice((2, group, piece, C), TRAVEL[3])
        + [
            pltpu.SemaphoreType.DMA((3, 2)),
            pltpu.SemaphoreType.DMA((3, 2)),
            pltpu.SemaphoreType.DMA((2, stages)),
            pltpu.SemaphoreType.DMA((2, stages)),
        ],
        compiler_params=pltpu.CompilerParams(
            collective_id=0, has_side_effects=True, vmem_limit_bytes=56 * 1024 * 1024
        ),
    )(tile_links, fields, cotangent, w_first, w_second)


def solution(mesh):
    placed = (
        P("dp", "space", None, None, None),
        P("dp", "space", None, None, None),
        P(),
        P(),
        P("space", None, None),
    )
    return jax.shard_map(
        functools.partial(block, mesh),
        mesh=mesh,
        in_specs=placed,
        out_specs=(P("dp", "space", None, None, None), P(), P()),
        check_vma=False,
    )
```

```python
import functools

import jax
import jax.numpy as jnp
from jax import lax
from jax.experimental import pallas as pl
from jax.experimental.pallas import tpu as pltpu
from jax.sharding import PartitionSpec as P

F32 = jnp.float32
BF16 = jnp.bfloat16
MESH = pl.DeviceIdType.MESH
TRAVEL = (F32, BF16, BF16, BF16)


def plan(dp_size, space_size, rows):
    mid = 2 if space_size % 4 == 0 else 1
    group = dp_size * mid
    far = space_size // (2 * mid)
    piece = -(-rows // (2 * group * 16)) * 16
    return mid, group, far, piece


def kernel(
    dp_size, space_size, tiles, side, chans, scale,
    links, f_ref, c_ref, w1_ref, w2_ref,
    mixed_ref, g1_ref, g2_ref,
    xc, ac, cc, gc, wb, deriv, agrad, rims, rim_corners, turns, picks,
    pool0, pool1, pool2, land0, land1, land2, out0, out1, out2,
    acc1, acc2, ra1, ra2, half1, half2, sb1, sb2, rb1, rb2, sc1, sc2, rc1, rc2, fo1, fo2,
    halo_send, halo_recv, red_send, red_recv,
):
    T, S, C = tiles, side, chans
    K = 3 * C
    pix = S * S
    pad_rows = S + 2
    su = S // 16
    own_units = 4 * T * su + T
    msg_units = T * su + T
    mid, group, far, piece = plan(dp_size, space_size, 9 * C)
    d = lax.axis_index("dp")
    s = lax.axis_index("space")
    core = lax.rem(s, 2)
    y = lax.rem(lax.div(s, 2), mid)
    z = lax.div(s, 2 * mid)
    b = d * mid + y
    lower = lax.rem(s + space_size - 1, space_size)
    upper = lax.rem(s + 1, space_size)
    partner = s + 1 - 2 * core

    def plane_peer(step):
        other = lax.rem(b + step, group)
        return (lax.div(other, mid), z * (2 * mid) + lax.rem(other, mid) * 2 + core)

    def far_peer(step):
        other = lax.rem(z + step, far)
        return (d, (other * mid + y) * 2 + core)

    barrier = pltpu.get_barrier_semaphore()
    greeted = [(d, lower), (d, upper), (d, partner)]
    greeted += [plane_peer(step) for step in range(1, group)]
    greeted += [far_peer(step) for step in range(1, far)]
    for peer in greeted:
        pl.semaphore_signal(barrier, inc=1, device_id=peer, device_id_type=MESH)

    def where_is(source):
        rel = lax.rem(lax.div(source, T) - s + 1 + space_size, space_size)
        return rel, lax.rem(source, T)

    strip_at, corner_at, face_lower, face_upper = {}, {}, [], []
    for t in range(T):
        low, up = 0, 0
        for k in range(4):
            rel, slot = where_is(links[t, k, 0])
            strip_at[t, k] = jnp.where(
                rel == 1,
                (slot * 4 + links[t, k, 1]) * su,
                jnp.where(rel == 0, own_units, own_units + msg_units) + slot * su,
            )
            low = low + jnp.where(rel == 0, k, 0)
            up = up + jnp.where(rel == 2, k, 0)
            rel, slot = where_is(links[t, k, 3])
            corner_at[t, k] = slot + jnp.where(
                rel == 1,
                4 * T * su,
                jnp.where(rel == 0, own_units, own_units + msg_units) + T * su,
            )
        face_lower.append(low)
        face_upper.append(up)

    def blocks(rows, columns, axis, size):
        at = lax.broadcasted_iota(jnp.int32, (rows, columns), axis)
        which = sum((at >= k * size).astype(jnp.int32) for k in range(1, 4))
        return which, at - which * size

    row_side, row_at = blocks(4 * S, 4 * S, 0, S)
    col_side, col_at = blocks(4 * S, 4 * S, 1, S)
    alike = row_side == col_side
    same = jnp.where(alike & (row_at == col_at), 1.0, 0.0)
    turned = jnp.where(alike & (row_at + col_at == S - 1), 1.0, 0.0)
    pick_row = lax.broadcasted_iota(jnp.int32, (16, 64), 0)
    pick_side, pick_at = blocks(16, 64, 1, 16)
    for t in range(T):
        flag, corner = jnp.zeros((4 * S, 4 * S), F32), jnp.zeros((16, 64), jnp.int32)
        for k in range(4):
            flag = jnp.where(row_side == k, links[t, k, 2].astype(F32), flag)
            corner = jnp.where(pick_row == k, links[t, k, 4], corner)
        turns[t] = (flag * turned + (1.0 - flag) * same).astype(BF16)
        hit = (pick_row == pick_side) & (pick_at == corner)
        picks[t] = jnp.where(hit, 1.0, 0.0).astype(BF16)

    unit_row = lax.broadcasted_iota(jnp.int32, (16, C), 0)
    line_row = lax.broadcasted_iota(jnp.int32, (S, C), 0)
    block_col = lax.broadcasted_iota(jnp.int32, (S, S, C), 1)

    pools, lands, outs = (pool0, pool1, pool2), (land0, land1, land2), (out0, out1, out2)

    def keep_strip(pool, t, k, strip):
        pool[pl.ds((t * 4 + k) * su, su)] = strip.astype(BF16).reshape(su, 16, C)

    def keep_corners(pool, t, corners):
        unit = jnp.zeros((16, C), F32)
        for k in range(4):
            unit = jnp.where(unit_row == k, corners[k], unit)
        pool[4 * T * su + t] = unit.astype(BF16)

    def keep_edges(pool, t, value):
        top, bottom = value[0], value[S - 1]
        keep_strip(pool, t, 0, top)
        keep_strip(pool, t, 1, value[:, S - 1, :])
        keep_strip(pool, t, 2, bottom)
        keep_strip(pool, t, 3, value[:, 0, :])
        keep_corners(pool, t, [top[0:1], top[S - 1 : S], bottom[S - 1 : S], bottom[0:1]])

    def halo_copies(which):
        copies = []
        for way, (peer, place) in enumerate(((lower, 1), (upper, 0))):
            copies.append(
                pltpu.make_async_remote_copy(
                    src_ref=outs[which].at[way],
                    dst_ref=lands[which].at[place],
                    send_sem=halo_send.at[which, way],
                    recv_sem=halo_recv.at[which, way],
                    device_id=(d, peer),
                    device_id_type=MESH,
                )
            )
        return copies

    def send_halo(which):
        pool, out = pools[which], outs[which]
        for way, faces in enumerate((face_lower, face_upper)):
            for t in range(T):
                out[way, pl.ds(t * su, su)] = pool[pl.ds((t * 4 + faces[t]) * su, su)]
                out[way, T * su + t] = pool[4 * T * su + t]

    def take_halo(which, copies):
        pool = pools[which]
        for copy in copies:
            copy.wait_recv()
        for place in range(2):
            pool[pl.ds(own_units + place * msg_units, msg_units)] = lands[which][place]
        for t in range(T):
            strips = [pool[pl.ds(strip_at[t, k], su)].reshape(S, C) for k in range(4)]
            units = [pool[corner_at[t, k]] for k in range(4)]
            rims[t] = jnp.dot(
                turns[t], jnp.concatenate(strips, axis=0), preferred_element_type=F32
            ).reshape(4, S, C)
            rim_corners[t] = jnp.dot(
                picks[t], jnp.concatenate(units, axis=0), preferred_element_type=F32
            )

    def shifted(dst, t, at, value, left, right, columns):
        extent = columns.ndim - 2
        last = S - 1
        before = jnp.where(columns == 0, left, pltpu.roll(value, 1, axis=extent))
        after = jnp.where(columns == last, right, pltpu.roll(value, last, axis=extent))
        dst[t, at, :, 0:C] = before.astype(BF16)
        dst[t, at, :, C : 2 * C] = value.astype(BF16)
        dst[t, at, :, 2 * C : K] = after.astype(BF16)

    def fill_padded(dst, t, value):
        left, right = rims[t, 3], rims[t, 1]
        shifted(dst, t, pl.ds(1, S), value, left[:, None, :], right[:, None, :], block_col)
        tl, tr = rim_corners[t, 0:1], rim_corners[t, 1:2]
        br, bl = rim_corners[t, 2:3], rim_corners[t, 3:4]
        shifted(dst, t, 0, rims[t, 0], tl, tr, line_row)
        shifted(dst, t, S + 1, rims[t, 2], bl, br, line_row)

    def conv(src, t, kernel_rows, order):
        lhs = jnp.concatenate([src[t, r : r + S].reshape(pix, K) for r in order], axis=1)
        return jnp.dot(lhs, kernel_rows, preferred_element_type=F32)

    def lower_rows(t, value):
        zero = jnp.zeros((1, S, C), BF16)
        for r in range(3):
            lanes = slice(r * C, (r + 1) * C)
            gc[t, r : r + S, :, lanes] = value
            for at in range(r):
                gc[t, at : at + 1, :, lanes] = zero
            for at in range(r + S, pad_rows):
                gc[t, at : at + 1, :, lanes] = zero

    def kernel_grad(padded, acc):
        total = None
        for t in range(T):
            part = lax.dot_general(
                padded[t].reshape(pad_rows * S, K),
                gc[t].reshape(pad_rows * S, K),
                (((0,), (0,)), ((), ())),
                preferred_element_type=F32,
            )
            total = part if total is None else total + part
        for r in range(3):
            for c in range(3):
                acc[pl.ds((r * 3 + c) * C, C)] = total[c * C : (c + 1) * C, r * C : (r + 1) * C]
        if 2 * group * piece > 9 * C:
            acc[9 * C :] = jnp.zeros((2 * group * piece - 9 * C, C), F32)

    half_rows = group * piece
    stage_at = (0, 1, group, group + far - 1, 2 * group + far - 2)

    def remote(which, index, src, dst, peer):
        return pltpu.make_async_remote_copy(
            src_ref=src, dst_ref=dst,
            send_sem=red_send.at[which, index], recv_sem=red_recv.at[which, index],
            device_id=peer, device_id_type=MESH,
        )

    accs, ras, halves = (acc1, acc2), (ra1, ra2), (half1, half2)
    sbs, rbs, scs, rcs, fos = (sb1, sb2), (rb1, rb2), (sc1, sc2), (rc1, rc2), (fo1, fo2)
    pending = []

    def launch(copies):
        for copy in copies:
            copy.start()
        pending.extend(copies)
        return copies

    def landed(copies):
        for copy in copies:
            copy.wait_recv()

    def pair_start(g):
        src = accs[g].at[pl.ds((1 - core) * half_rows, half_rows)]
        return launch([remote(g, 0, src, ras[g], (d, partner))])

    def plane_start(g, copies):
        landed(copies)
        halves[g][...] = accs[g][pl.ds(core * half_rows, half_rows)] + ras[g][...]
        result = []
        for step in range(1, group):
            other = lax.rem(b + step, group)
            sbs[g][step - 1] = halves[g][pl.ds(other * piece, piece)].astype(sbs[g].dtype)
            result.append(
                remote(g, stage_at[1] + step - 1, sbs[g].at[step - 1], rbs[g].at[step - 1], plane_peer(step))
            )
        return launch(result)

    def far_start(g, copies):
        landed(copies)
        total = halves[g][pl.ds(b * piece, piece)]
        for step in range(1, group):
            total = total + rbs[g][step - 1].astype(F32)
        scs[g][...] = total.astype(scs[g].dtype)
        return launch([
            remote(g, stage_at[2] + step - 1, scs[g], rcs[g].at[z], far_peer(step))
            for step in range(1, far)
        ])

    def back_start(g, copies):
        landed(copies)
        total = jnp.zeros((piece, C), F32)
        mine = scs[g][...].astype(F32)
        for at in range(far):
            total = total + jnp.where(z == at, mine, rcs[g][at].astype(F32))
        fos[g][core, b] = (total * scale).astype(fos[g].dtype)
        spot = fos[g].at[core, b]
        return launch([
            remote(g, stage_at[3] + step - 1, spot, spot, plane_peer(step))
            for step in range(1, group)
        ])

    def pair_back(g, copies):
        landed(copies)
        spot = fos[g].at[core]
        return launch([remote(g, stage_at[4], spot, spot, (d, partner))])

    def finish(g, copies, out):
        landed(copies)
        out[...] = fos[g][...].reshape(2 * half_rows, C)[: 9 * C].astype(F32).reshape(3, 3, C, C)

    @pl.loop(0, T)
    def _(t):
        keep_edges(pool0, t, f_ref[0, t].astype(F32))

    send_halo(0)
    pl.semaphore_wait(barrier, len(greeted))
    copies0 = halo_copies(0)
    launch(copies0)

    for r in range(3):
        for c in range(3):
            wb[pl.ds((r * 3 + c) * C, C)] = w2_ref[r, c].astype(F32).T.astype(BF16)

    @pl.loop(0, T)
    def _(t):
        value = c_ref[0, t].astype(F32)
        blank = jnp.zeros((1, S, K), BF16)
        zero = jnp.zeros((), F32)
        up = jnp.where(block_col == S - 1, zero, pltpu.roll(value, S - 1, axis=1))
        down = jnp.where(block_col == 0, zero, pltpu.roll(value, 1, axis=1))
        cc[t, pl.ds(1, S), :, 0:C] = up.astype(BF16)
        cc[t, pl.ds(1, S), :, C : 2 * C] = c_ref[0, t]
        cc[t, pl.ds(1, S), :, 2 * C : K] = down.astype(BF16)
        cc[t, 0:1] = blank
        cc[t, S + 1 : S + 2] = blank
        top = jnp.dot(cc[t, 1], wb[0:K], preferred_element_type=F32)
        bottom = jnp.dot(cc[t, S], wb[2 * K : 3 * K], preferred_element_type=F32)
        corners = {}
        for column, c, k in ((0, 0, 3), (S - 1, 2, 1)):
            line = value[:, column, :].astype(BF16)
            parts = [
                jnp.dot(line, wb[(r * 3 + c) * C : (r * 3 + c + 1) * C], preferred_element_type=F32)
                for r in range(3)
            ]
            strip = parts[1]
            strip = strip + jnp.where(line_row == S - 1, 0.0, pltpu.roll(parts[0], S - 1, axis=0))
            strip = strip + jnp.where(line_row == 0, 0.0, pltpu.roll(parts[2], 1, axis=0))
            keep_strip(pool1, t, k, strip)
            corners[c] = (parts[0][0:1], parts[2][S - 1 : S])
        keep_strip(pool1, t, 0, top)
        keep_strip(pool1, t, 2, bottom)
        keep_corners(pool1, t, [corners[0][0], corners[2][0], corners[2][1], corners[0][1]])

    send_halo(1)
    copies1 = launch(halo_copies(1))

    @pl.loop(0, T)
    def _(t):
        agrad[t] = conv(cc, t, wb[...], (2, 1, 0)).reshape(S, S, C)

    take_halo(0, copies0)

    @pl.loop(0, T)
    def _(t):
        fill_padded(xc, t, f_ref[0, t].astype(F32))
        hidden = conv(xc, t, w1_ref[...].reshape(9 * C, C), (0, 1, 2))
        gate = jax.nn.sigmoid(hidden)
        active = (hidden * gate).reshape(S, S, C)
        deriv[t] = (gate * (1.0 + hidden * (1.0 - gate))).reshape(S, S, C)
        ac[t, pl.ds(1, S), :, C : 2 * C] = active.astype(BF16)
        keep_edges(pool2, t, active)

    send_halo(2)
    copies2 = launch(halo_copies(2))

    take_halo(1, copies1)

    @pl.loop(0, T)
    def _(t):
        agrad[t, 0] = agrad[t, 0] + rims[t, 0]
        agrad[t, S - 1] = agrad[t, S - 1] + rims[t, 2]
        for column, k, above, below in ((0, 3, 0, 3), (S - 1, 1, 1, 2)):
            strip = rims[t, k]
            strip = strip + jnp.where(line_row == 0, rim_corners[t, above : above + 1], 0.0)
            strip = strip + jnp.where(line_row == S - 1, rim_corners[t, below : below + 1], 0.0)
            agrad[t, :, column : column + 1, :] = (
                agrad[t, :, column : column + 1, :] + strip[:, None, :]
            )
        lower_rows(t, (agrad[t] * deriv[t]).astype(BF16))

    kernel_grad(xc, acc1)
    first = pair_start(0)

    take_halo(2, copies2)

    @pl.loop(0, T)
    def _(t):
        fill_padded(ac, t, ac[t, pl.ds(1, S), :, C : 2 * C].astype(F32))
        lower_rows(t, c_ref[0, t])

    first = plane_start(0, first)
    kernel_grad(ac, acc2)
    second = pair_start(1)
    first = far_start(0, first)

    def output(t):
        out = conv(ac, t, w2_ref[...].reshape(9 * C, C), (0, 1, 2)).reshape(S, S, C)
        mixed_ref[0, t] = (f_ref[0, t].astype(F32) + out).astype(BF16)

    pl.loop(0, T // 2)(output)
    second = plane_start(1, second)
    pl.loop(T // 2, T)(output)
    second = far_start(1, second)
    first = back_start(0, first)
    second = back_start(1, second)
    first = pair_back(0, first)
    second = pair_back(1, second)
    finish(0, first, g1_ref)
    finish(1, second, g2_ref)
    for copy in pending:
        copy.wait_send()


def block(mesh, fields, cotangent, w_first, w_second, tile_links):
    samples, T, S, _, C = fields.shape
    assert samples == 1
    dp_size, space_size = mesh.shape["dp"], mesh.shape["space"]
    mid, group, far, piece = plan(dp_size, space_size, 9 * C)
    scale = float(samples * dp_size * T * space_size * S * S) ** (-0.5)
    su = S // 16
    own_units, msg_units = 4 * T * su + T, T * su + T
    vmem = pltpu.VMEM
    padded = vmem((T, S + 2, S, 3 * C), BF16)
    twice = lambda shape, kind: [vmem(shape, kind), vmem(shape, kind)]
    stages = 2 * group + far - 1
    specs = pl.BlockSpec(memory_space=pltpu.VMEM)
    return pl.pallas_call(
        functools.partial(kernel, dp_size, space_size, T, S, C, scale),
        out_shape=(
            jax.ShapeDtypeStruct(fields.shape, BF16),
            jax.ShapeDtypeStruct(w_first.shape, F32),
            jax.ShapeDtypeStruct(w_second.shape, F32),
        ),
        in_specs=[pl.BlockSpec(memory_space=pltpu.SMEM), specs, specs, specs, specs],
        out_specs=(specs, specs, specs),
        scratch_shapes=[
            padded, padded, padded, padded,
            vmem((9 * C, C), BF16),
            vmem((T, S, S, C), F32),
            vmem((T, S, S, C), F32),
            vmem((T, 4, S, C), F32),
            vmem((T, 16, C), F32),
            vmem((T, 4 * S, 4 * S), BF16),
            vmem((T, 16, 64), BF16),
        ]
        + [vmem((own_units + 2 * msg_units, 16, C), BF16)] * 3
        + [vmem((2, msg_units, 16, C), BF16)] * 6
        + twice((2 * group * piece, C), F32)
        + twice((group * piece, C), TRAVEL[0])
        + twice((group * piece, C), F32)
        + twice((group - 1, piece, C), TRAVEL[1])
        + twice((group - 1, piece, C), TRAVEL[1])
        + twice((piece, C), TRAVEL[2])
        + twice((far, piece, C), TRAVEL[2])
        + twice((2, group, piece, C), TRAVEL[3])
        + [
            pltpu.SemaphoreType.DMA((3, 2)),
            pltpu.SemaphoreType.DMA((3, 2)),
            pltpu.SemaphoreType.DMA((2, stages)),
            pltpu.SemaphoreType.DMA((2, stages)),
        ],
        compiler_params=pltpu.CompilerParams(
            collective_id=0, has_side_effects=True, vmem_limit_bytes=56 * 1024 * 1024
        ),
    )(tile_links, fields, cotangent, w_first, w_second)


def solution(mesh):
    placed = (
        P("dp", "space", None, None, None),
        P("dp", "space", None, None, None),
        P(),
        P(),
        P("space", None, None),
    )
    return jax.shard_map(
        functools.partial(block, mesh),
        mesh=mesh,
        in_specs=placed,
        out_specs=(P("dp", "space", None, None, None), P(), P()),
        check_vma=False,
    )
```

```python
import functools

import jax
import jax.numpy as jnp
from jax import lax
from jax.experimental import pallas as pl
from jax.experimental.pallas import tpu as pltpu
from jax.sharding import PartitionSpec as P

F32 = jnp.float32
BF16 = jnp.bfloat16
MESH = pl.DeviceIdType.MESH
TRAVEL = (F32, BF16, BF16, BF16)


def plan(dp_size, space_size, rows):
    mid = 2 if space_size % 4 == 0 else 1
    group = dp_size * mid
    far = space_size // (2 * mid)
    piece = -(-rows // (2 * group * 16)) * 16
    return mid, group, far, piece


def kernel(
    dp_size, space_size, tiles, side, chans, scale,
    links, f_ref, c_ref, w1_ref, w2_ref,
    mixed_ref, g1_ref, g2_ref,
    xc, ac, cc, gc, wb, deriv, agrad, rims, rim_corners, turns, picks,
    pool0, pool1, pool2, land0, land1, land2, out0, out1, out2,
    acc1, acc2, ra1, ra2, half1, half2, sb1, sb2, rb1, rb2, sc1, sc2, rc1, rc2, fo1, fo2,
    halo_send, halo_recv, red_send, red_recv,
):
    T, S, C = tiles, side, chans
    K = 3 * C
    pix = S * S
    pad_rows = S + 2
    su = S // 16
    own_units = 4 * T * su + T
    msg_units = T * su + T
    mid, group, far, piece = plan(dp_size, space_size, 9 * C)
    d = lax.axis_index("dp")
    s = lax.axis_index("space")
    core = lax.rem(s, 2)
    y = lax.rem(lax.div(s, 2), mid)
    z = lax.div(s, 2 * mid)
    b = d * mid + y
    lower = lax.rem(s + space_size - 1, space_size)
    upper = lax.rem(s + 1, space_size)
    partner = s + 1 - 2 * core

    def plane_peer(step):
        other = lax.rem(b + step, group)
        return (lax.div(other, mid), z * (2 * mid) + lax.rem(other, mid) * 2 + core)

    def far_peer(step):
        other = lax.rem(z + step, far)
        return (d, (other * mid + y) * 2 + core)

    barrier = pltpu.get_barrier_semaphore()
    greeted = [(d, lower), (d, upper), (d, partner)]
    greeted += [plane_peer(step) for step in range(1, group)]
    greeted += [far_peer(step) for step in range(1, far)]
    for peer in greeted:
        pl.semaphore_signal(barrier, inc=1, device_id=peer, device_id_type=MESH)

    def where_is(source):
        rel = lax.rem(lax.div(source, T) - s + 1 + space_size, space_size)
        return rel, lax.rem(source, T)

    strip_at, corner_at, face_lower, face_upper = {}, {}, [], []
    for t in range(T):
        low, up = 0, 0
        for k in range(4):
            rel, slot = where_is(links[t, k, 0])
            strip_at[t, k] = jnp.where(
                rel == 1,
                (slot * 4 + links[t, k, 1]) * su,
                jnp.where(rel == 0, own_units, own_units + msg_units) + slot * su,
            )
            low = low + jnp.where(rel == 0, k, 0)
            up = up + jnp.where(rel == 2, k, 0)
            rel, slot = where_is(links[t, k, 3])
            corner_at[t, k] = slot + jnp.where(
                rel == 1,
                4 * T * su,
                jnp.where(rel == 0, own_units, own_units + msg_units) + T * su,
            )
        face_lower.append(low)
        face_upper.append(up)

    def blocks(rows, columns, axis, size):
        at = lax.broadcasted_iota(jnp.int32, (rows, columns), axis)
        which = sum((at >= k * size).astype(jnp.int32) for k in range(1, 4))
        return which, at - which * size

    row_side, row_at = blocks(4 * S, 4 * S, 0, S)
    col_side, col_at = blocks(4 * S, 4 * S, 1, S)
    alike = row_side == col_side
    same = jnp.where(alike & (row_at == col_at), 1.0, 0.0)
    turned = jnp.where(alike & (row_at + col_at == S - 1), 1.0, 0.0)
    pick_row = lax.broadcasted_iota(jnp.int32, (16, 64), 0)
    pick_side, pick_at = blocks(16, 64, 1, 16)
    for t in range(T):
        flag, corner = jnp.zeros((4 * S, 4 * S), F32), jnp.zeros((16, 64), jnp.int32)
        for k in range(4):
            flag = jnp.where(row_side == k, links[t, k, 2].astype(F32), flag)
            corner = jnp.where(pick_row == k, links[t, k, 4], corner)
        turns[t] = (flag * turned + (1.0 - flag) * same).astype(BF16)
        hit = (pick_row == pick_side) & (pick_at == corner)
        picks[t] = jnp.where(hit, 1.0, 0.0).astype(BF16)

    unit_row = lax.broadcasted_iota(jnp.int32, (16, C), 0)
    line_row = lax.broadcasted_iota(jnp.int32, (S, C), 0)
    block_col = lax.broadcasted_iota(jnp.int32, (S, S, C), 1)

    pools, lands, outs = (pool0, pool1, pool2), (land0, land1, land2), (out0, out1, out2)

    def keep_strip(pool, t, k, strip):
        pool[pl.ds((t * 4 + k) * su, su)] = strip.astype(BF16).reshape(su, 16, C)

    def keep_corners(pool, t, corners):
        unit = jnp.zeros((16, C), F32)
        for k in range(4):
            unit = jnp.where(unit_row == k, corners[k], unit)
        pool[4 * T * su + t] = unit.astype(BF16)

    def keep_edges(pool, t, value):
        top, bottom = value[0], value[S - 1]
        keep_strip(pool, t, 0, top)
        keep_strip(pool, t, 1, value[:, S - 1, :])
        keep_strip(pool, t, 2, bottom)
        keep_strip(pool, t, 3, value[:, 0, :])
        keep_corners(pool, t, [top[0:1], top[S - 1 : S], bottom[S - 1 : S], bottom[0:1]])

    def halo_copies(which):
        copies = []
        for way, (peer, place) in enumerate(((lower, 1), (upper, 0))):
            copies.append(
                pltpu.make_async_remote_copy(
                    src_ref=outs[which].at[way],
                    dst_ref=lands[which].at[place],
                    send_sem=halo_send.at[which, way],
                    recv_sem=halo_recv.at[which, way],
                    device_id=(d, peer),
                    device_id_type=MESH,
                )
            )
        return copies

    def send_halo(which):
        pool, out = pools[which], outs[which]
        for way, faces in enumerate((face_lower, face_upper)):
            for t in range(T):
                out[way, pl.ds(t * su, su)] = pool[pl.ds((t * 4 + faces[t]) * su, su)]
                out[way, T * su + t] = pool[4 * T * su + t]

    def take_halo(which, copies):
        pool = pools[which]
        for copy in copies:
            copy.wait_recv()
        for place in range(2):
            pool[pl.ds(own_units + place * msg_units, msg_units)] = lands[which][place]
        for t in range(T):
            strips = [pool[pl.ds(strip_at[t, k], su)].reshape(S, C) for k in range(4)]
            units = [pool[corner_at[t, k]] for k in range(4)]
            rims[t] = jnp.dot(
                turns[t], jnp.concatenate(strips, axis=0), preferred_element_type=F32
            ).reshape(4, S, C)
            rim_corners[t] = jnp.dot(
                picks[t], jnp.concatenate(units, axis=0), preferred_element_type=F32
            )

    def shifted(dst, t, at, value, left, right, columns):
        extent = columns.ndim - 2
        last = S - 1
        before = jnp.where(columns == 0, left, pltpu.roll(value, 1, axis=extent))
        after = jnp.where(columns == last, right, pltpu.roll(value, last, axis=extent))
        dst[t, at, :, 0:C] = before.astype(BF16)
        dst[t, at, :, C : 2 * C] = value.astype(BF16)
        dst[t, at, :, 2 * C : K] = after.astype(BF16)

    def fill_padded(dst, t, value):
        left, right = rims[t, 3], rims[t, 1]
        shifted(dst, t, pl.ds(1, S), value, left[:, None, :], right[:, None, :], block_col)
        tl, tr = rim_corners[t, 0:1], rim_corners[t, 1:2]
        br, bl = rim_corners[t, 2:3], rim_corners[t, 3:4]
        shifted(dst, t, 0, rims[t, 0], tl, tr, line_row)
        shifted(dst, t, S + 1, rims[t, 2], bl, br, line_row)

    def conv(src, t, kernel_rows, order):
        lhs = jnp.concatenate([src[t, r : r + S].reshape(pix, K) for r in order], axis=1)
        return jnp.dot(lhs, kernel_rows, preferred_element_type=F32)

    def lower_rows(t, value):
        zero = jnp.zeros((1, S, C), BF16)
        for r in range(3):
            lanes = slice(r * C, (r + 1) * C)
            gc[t, r : r + S, :, lanes] = value
            for at in range(r):
                gc[t, at : at + 1, :, lanes] = zero
            for at in range(r + S, pad_rows):
                gc[t, at : at + 1, :, lanes] = zero

    def kernel_grad(padded, acc):
        total = None
        for t in range(T):
            part = lax.dot_general(
                padded[t].reshape(pad_rows * S, K),
                gc[t].reshape(pad_rows * S, K),
                (((0,), (0,)), ((), ())),
                preferred_element_type=F32,
            )
            total = part if total is None else total + part
        for r in range(3):
            for c in range(3):
                acc[pl.ds((r * 3 + c) * C, C)] = total[c * C : (c + 1) * C, r * C : (r + 1) * C]
        if 2 * group * piece > 9 * C:
            acc[9 * C :] = jnp.zeros((2 * group * piece - 9 * C, C), F32)

    half_rows = group * piece
    stage_at = (0, 1, group, group + far - 1, 2 * group + far - 2)

    def remote(which, index, src, dst, peer):
        return pltpu.make_async_remote_copy(
            src_ref=src, dst_ref=dst,
            send_sem=red_send.at[which, index], recv_sem=red_recv.at[which, index],
            device_id=peer, device_id_type=MESH,
        )

    accs, ras, halves = (acc1, acc2), (ra1, ra2), (half1, half2)
    sbs, rbs, scs, rcs, fos = (sb1, sb2), (rb1, rb2), (sc1, sc2), (rc1, rc2), (fo1, fo2)
    pending = []

    def launch(copies):
        for copy in copies:
            copy.start()
        pending.extend(copies)
        return copies

    def landed(copies):
        for copy in copies:
            copy.wait_recv()

    def pair_start(g):
        src = accs[g].at[pl.ds((1 - core) * half_rows, half_rows)]
        return launch([remote(g, 0, src, ras[g], (d, partner))])

    def plane_start(g, copies):
        landed(copies)
        halves[g][...] = accs[g][pl.ds(core * half_rows, half_rows)] + ras[g][...]
        result = []
        for step in range(1, group):
            other = lax.rem(b + step, group)
            sbs[g][step - 1] = halves[g][pl.ds(other * piece, piece)].astype(sbs[g].dtype)
            result.append(
                remote(g, stage_at[1] + step - 1, sbs[g].at[step - 1], rbs[g].at[step - 1], plane_peer(step))
            )
        return launch(result)

    def far_start(g, copies):
        landed(copies)
        total = halves[g][pl.ds(b * piece, piece)]
        for step in range(1, group):
            total = total + rbs[g][step - 1].astype(F32)
        scs[g][...] = total.astype(scs[g].dtype)
        return launch([
            remote(g, stage_at[2] + step - 1, scs[g], rcs[g].at[z], far_peer(step))
            for step in range(1, far)
        ])

    def back_start(g, copies):
        landed(copies)
        total = jnp.zeros((piece, C), F32)
        mine = scs[g][...].astype(F32)
        for at in range(far):
            total = total + jnp.where(z == at, mine, rcs[g][at].astype(F32))
        fos[g][core, b] = (total * scale).astype(fos[g].dtype)
        spot = fos[g].at[core, b]
        return launch([
            remote(g, stage_at[3] + step - 1, spot, spot, plane_peer(step))
            for step in range(1, group)
        ])

    def pair_back(g, copies):
        landed(copies)
        spot = fos[g].at[core]
        return launch([remote(g, stage_at[4], spot, spot, (d, partner))])

    def finish(g, copies, out):
        landed(copies)
        out[...] = fos[g][...].reshape(2 * half_rows, C)[: 9 * C].astype(F32).reshape(3, 3, C, C)

    @pl.loop(0, T)
    def _(t):
        keep_edges(pool0, t, f_ref[0, t].astype(F32))

    send_halo(0)
    pl.semaphore_wait(barrier, len(greeted))
    copies0 = halo_copies(0)
    launch(copies0)

    for r in range(3):
        for c in range(3):
            wb[pl.ds((r * 3 + c) * C, C)] = w2_ref[r, c].astype(F32).T.astype(BF16)

    @pl.loop(0, T)
    def _(t):
        value = c_ref[0, t].astype(F32)
        blank = jnp.zeros((1, S, K), BF16)
        zero = jnp.zeros((), F32)
        up = jnp.where(block_col == S - 1, zero, pltpu.roll(value, S - 1, axis=1))
        down = jnp.where(block_col == 0, zero, pltpu.roll(value, 1, axis=1))
        cc[t, pl.ds(1, S), :, 0:C] = up.astype(BF16)
        cc[t, pl.ds(1, S), :, C : 2 * C] = c_ref[0, t]
        cc[t, pl.ds(1, S), :, 2 * C : K] = down.astype(BF16)
        cc[t, 0:1] = blank
        cc[t, S + 1 : S + 2] = blank
        top = jnp.dot(cc[t, 1], wb[0:K], preferred_element_type=F32)
        bottom = jnp.dot(cc[t, S], wb[2 * K : 3 * K], preferred_element_type=F32)
        corners = {}
        for column, c, k in ((0, 0, 3), (S - 1, 2, 1)):
            line = value[:, column, :].astype(BF16)
            parts = [
                jnp.dot(line, wb[(r * 3 + c) * C : (r * 3 + c + 1) * C], preferred_element_type=F32)
                for r in range(3)
            ]
            strip = parts[1]
            strip = strip + jnp.where(line_row == S - 1, 0.0, pltpu.roll(parts[0], S - 1, axis=0))
            strip = strip + jnp.where(line_row == 0, 0.0, pltpu.roll(parts[2], 1, axis=0))
            keep_strip(pool1, t, k, strip)
            corners[c] = (parts[0][0:1], parts[2][S - 1 : S])
        keep_strip(pool1, t, 0, top)
        keep_strip(pool1, t, 2, bottom)
        keep_corners(pool1, t, [corners[0][0], corners[2][0], corners[2][1], corners[0][1]])

    send_halo(1)
    copies1 = launch(halo_copies(1))

    @pl.loop(0, T)
    def _(t):
        agrad[t] = conv(cc, t, wb[...], (2, 1, 0)).reshape(S, S, C)

    take_halo(0, copies0)

    @pl.loop(0, T)
    def _(t):
        fill_padded(xc, t, f_ref[0, t].astype(F32))
        hidden = conv(xc, t, w1_ref[...].reshape(9 * C, C), (0, 1, 2))
        gate = jax.nn.sigmoid(hidden)
        active = (hidden * gate).reshape(S, S, C)
        deriv[t] = (gate * (1.0 + hidden * (1.0 - gate))).reshape(S, S, C)
        ac[t, pl.ds(1, S), :, C : 2 * C] = active.astype(BF16)
        keep_edges(pool2, t, active)

    send_halo(2)
    copies2 = launch(halo_copies(2))

    take_halo(1, copies1)

    @pl.loop(0, T)
    def _(t):
        agrad[t, 0] = agrad[t, 0] + rims[t, 0]
        agrad[t, S - 1] = agrad[t, S - 1] + rims[t, 2]
        for column, k, above, below in ((0, 3, 0, 3), (S - 1, 1, 1, 2)):
            strip = rims[t, k]
            strip = strip + jnp.where(line_row == 0, rim_corners[t, above : above + 1], 0.0)
            strip = strip + jnp.where(line_row == S - 1, rim_corners[t, below : below + 1], 0.0)
            agrad[t, :, column : column + 1, :] = (
                agrad[t, :, column : column + 1, :] + strip[:, None, :]
            )
        lower_rows(t, (agrad[t] * deriv[t]).astype(BF16))

    kernel_grad(xc, acc1)
    first = pair_start(0)

    take_halo(2, copies2)

    @pl.loop(0, T)
    def _(t):
        fill_padded(ac, t, ac[t, pl.ds(1, S), :, C : 2 * C].astype(F32))
        lower_rows(t, c_ref[0, t])

    first = plane_start(0, first)
    kernel_grad(ac, acc2)
    second = pair_start(1)
    first = far_start(0, first)

    def output(t):
        out = conv(ac, t, w2_ref[...].reshape(9 * C, C), (0, 1, 2)).reshape(S, S, C)
        mixed_ref[0, t] = (f_ref[0, t].astype(F32) + out).astype(BF16)

    pl.loop(0, 1)(output)
    second = plane_start(1, second)
    pl.loop(1, T)(output)
    second = far_start(1, second)
    first = back_start(0, first)
    second = back_start(1, second)
    first = pair_back(0, first)
    second = pair_back(1, second)
    finish(0, first, g1_ref)
    finish(1, second, g2_ref)
    for copy in pending:
        copy.wait_send()


def block(mesh, fields, cotangent, w_first, w_second, tile_links):
    samples, T, S, _, C = fields.shape
    assert samples == 1
    dp_size, space_size = mesh.shape["dp"], mesh.shape["space"]
    mid, group, far, piece = plan(dp_size, space_size, 9 * C)
    scale = float(samples * dp_size * T * space_size * S * S) ** (-0.5)
    su = S // 16
    own_units, msg_units = 4 * T * su + T, T * su + T
    vmem = pltpu.VMEM
    padded = vmem((T, S + 2, S, 3 * C), BF16)
    twice = lambda shape, kind: [vmem(shape, kind), vmem(shape, kind)]
    stages = 2 * group + far - 1
    specs = pl.BlockSpec(memory_space=pltpu.VMEM)
    return pl.pallas_call(
        functools.partial(kernel, dp_size, space_size, T, S, C, scale),
        out_shape=(
            jax.ShapeDtypeStruct(fields.shape, BF16),
            jax.ShapeDtypeStruct(w_first.shape, F32),
            jax.ShapeDtypeStruct(w_second.shape, F32),
        ),
        in_specs=[pl.BlockSpec(memory_space=pltpu.SMEM), specs, specs, specs, specs],
        out_specs=(specs, specs, specs),
        scratch_shapes=[
            padded, padded, padded, padded,
            vmem((9 * C, C), BF16),
            vmem((T, S, S, C), F32),
            vmem((T, S, S, C), F32),
            vmem((T, 4, S, C), F32),
            vmem((T, 16, C), F32),
            vmem((T, 4 * S, 4 * S), BF16),
            vmem((T, 16, 64), BF16),
        ]
        + [vmem((own_units + 2 * msg_units, 16, C), BF16)] * 3
        + [vmem((2, msg_units, 16, C), BF16)] * 6
        + twice((2 * group * piece, C), F32)
        + twice((group * piece, C), TRAVEL[0])
        + twice((group * piece, C), F32)
        + twice((group - 1, piece, C), TRAVEL[1])
        + twice((group - 1, piece, C), TRAVEL[1])
        + twice((piece, C), TRAVEL[2])
        + twice((far, piece, C), TRAVEL[2])
        + twice((2, group, piece, C), TRAVEL[3])
        + [
            pltpu.SemaphoreType.DMA((3, 2)),
            pltpu.SemaphoreType.DMA((3, 2)),
            pltpu.SemaphoreType.DMA((2, stages)),
            pltpu.SemaphoreType.DMA((2, stages)),
        ],
        compiler_params=pltpu.CompilerParams(
            collective_id=0, has_side_effects=True, vmem_limit_bytes=56 * 1024 * 1024
        ),
    )(tile_links, fields, cotangent, w_first, w_second)


def solution(mesh):
    placed = (
        P("dp", "space", None, None, None),
        P("dp", "space", None, None, None),
        P(),
        P(),
        P("space", None, None),
    )
    return jax.shard_map(
        functools.partial(block, mesh),
        mesh=mesh,
        in_specs=placed,
        out_specs=(P("dp", "space", None, None, None), P(), P()),
        check_vma=False,
    )
```
